128 devices in a mesh: tok: 8 (over x_hi, z), feat: 16 (over y, x_lo, core).
Axes of the slice: x: 4 (x_hi: 2, x_lo: 2; x = x_hi * 2 + x_lo), y: 4, z: 4, core: 2. Of those that a mesh axis runs over, the one named last changes fastest.
Arguments:
- activations: bfloat16 [32768, 28672], P('tok', 'feat'), may hold values from -6 to 6
- out_grads: bfloat16 [32768, 8192], P('tok', 'feat'), may hold values from -6 to 6
- query_in: bfloat16 [16, 32, 28672], P('tok', None, 'feat'), may hold values from -0.03125 to 0.03125
- query_out: bfloat16 [16, 32, 8192], P('tok', None, 'feat'), may hold values from -0.0625 to 0.0625
Outputs:
- influence: float32 [16, 32768], P(None, ('tok', 'feat'))
The draws below stay inside these ranges and needn't reach their ends.
All inputs are finite; a program needn't handle non-finite values.
Results may differ from the reference program's by a relative error of at most 0.0003.
Values may be sent and summed in bfloat16 or wider, within the bound.
No kernel may reach another device: no remote copies, remote signals or barrier semaphores. Data moves between devices by JAX's collectives and lax.ppermute only.
A program may use at most 128 MiB of HBM per device.

```python
import jax
import jax.numpy as jnp
from jax import lax

FIN = 28672
DOUT = 8192
RANK = 32
TOKENS = 32768
QUERIES = 16


def level_of(own_key, dims, cuts, smallest, top_value):
    factor_of = 1.0
    for position, shards_of in cuts:
        draws = jax.random.uniform(jax.random.fold_in(jax.random.fold_in(own_key, 6), position), (shards_of,), jnp.float32, smallest / len(cuts), top_value / len(cuts))
        factor_of = factor_of * jnp.repeat(jnp.exp(draws), dims[position] // shards_of).reshape((-1,) + (1,) * (len(dims) - 1 - position))
    return factor_of


def scatter_about(stream_key, shape, deviation, limit, cuts=(), held_as=jnp.bfloat16):
    array = jax.random.normal(stream_key, shape, jnp.float32) * deviation
    if len(cuts) > 0:
        array = level_of(stream_key, shape, cuts, -0.22, 0.18) * array
    return jnp.clip(array, min=-limit, max=limit).astype(held_as)


def setup_inputs(seed: int = 0) -> dict:
    key_of = jax.random.split(jax.random.key(seed), 5)
    activations = scatter_about(key_of[0], (TOKENS, FIN), 1.0, 6.0, ((0, 8), (1, 16)))
    out_grads = scatter_about(key_of[1], (TOKENS, DOUT), 1.0, 6.0, ((0, 8), (1, 16)))
    query_in = scatter_about(key_of[2], (QUERIES, RANK, FIN), FIN ** -0.5, 0.03125, ((0, 8), (2, 16)))
    query_out = scatter_about(key_of[3], (QUERIES, RANK, DOUT), DOUT ** -0.5, 0.0625, ((0, 8), (2, 16)))
    return {"activations": activations, "out_grads": out_grads, "query_in": query_in, "query_out": query_out}


def reference(activations, out_grads, query_in, query_out):
    in_flat = query_in.reshape(QUERIES * RANK, FIN)
    out_flat = query_out.reshape(QUERIES * RANK, DOUT)
    in_proj = lax.dot_general(activations, in_flat, (((1,), (1,)), ((), ())), preferred_element_type=jnp.float32)
    out_proj = lax.dot_general(out_grads, out_flat, (((1,), (1,)), ((), ())), preferred_element_type=jnp.float32)
    product = (in_proj * out_proj).reshape(TOKENS, QUERIES, RANK)
    return jnp.sum(product, axis=2).T
```

```python
import functools

import jax
import jax.numpy as jnp
from jax import lax
from jax.experimental import pallas as pl
from jax.experimental.pallas import tpu as pltpu
from jax.sharding import PartitionSpec as P

RANK = 32
BLOCK = 256
SPAN = 173.25
VMEM = 24 * 2**20
NT = (((1,), (1,)), ((), ()))

G1, G0, X = 2, 1, 0
ORDERS = ((X, G0, G1), (G0, G1, X), (G1, X, G0))


def gray(y):
    return y ^ (y >> 1)


def block_of(feat, j, core_bit):
    y = gray(gray(feat >> 2) ^ (j >> 1))
    return (y << 2) | ((((feat >> 1) & 1) ^ (j & 1)) << 1) | ((feat & 1) ^ core_bit)


def feat_pairs(bit):
    if bit == "core":
        return [(s, s ^ 1) for s in range(16)]
    if bit == X:
        return [(s, s ^ 2) for s in range(16)]
    flip = 1 if bit == G0 else 2
    return [(s, (gray(gray(s >> 2) ^ flip) << 2) | (s & 3)) for s in range(16)]


def send_feat(value, bit):
    return lax.ppermute(value, "feat", feat_pairs(bit))


def encode(value):
    rows, cols = value.shape
    grouped = jnp.abs(value).reshape(rows // RANK, RANK, cols)
    top = jnp.max(grouped, axis=1, keepdims=True)
    scale = (top * 1.01 + 1e-35).astype(jnp.bfloat16).astype(jnp.float32)
    part = grouped * (1.0 / scale) + 1e-30
    root = (part * lax.rsqrt(part)).reshape(rows, cols)
    code = jnp.exp(root * SPAN - SPAN / 2)
    return jnp.where(value < 0, -code, code).astype(jnp.bfloat16), scale.reshape(rows // RANK, cols)


def decode(code, scale):
    rows, cols = code.shape
    code = code.astype(jnp.float32)
    root = jnp.log(jnp.abs(code)) * (1.0 / SPAN) + 0.5
    size = (root * root).reshape(rows // RANK, RANK, cols) * scale.reshape(rows // RANK, 1, cols)
    size = size.reshape(rows, cols)
    return jnp.where(code < 0, -size, size)


def put(ref, pos, value):
    rows, cols = value.shape
    code, scale = encode(value)
    ref[pos, :rows, :] = code
    row = lax.broadcasted_iota(jnp.int32, (16, cols), 0)
    packed = jnp.zeros((16, cols), jnp.float32)
    for g in range(rows // RANK):
        packed = jnp.where(row == g, scale[g : g + 1, :], packed)
    ref[pos, rows : rows + 16, :] = packed.astype(jnp.bfloat16)


def get(ref, pos):
    rows = ref.shape[1] - 16
    scale = ref[pos, rows : rows + 16, :].astype(jnp.float32)[: rows // RANK, :]
    return decode(ref[pos, :rows, :], scale)


def project(act_ref, grad_ref, factor_refs):
    n_in = act_ref.shape[1]
    q_in = jnp.concatenate([f[:, :n_in] for f in factor_refs], axis=0)
    q_out = jnp.concatenate([f[:, n_in:] for f in factor_refs], axis=0)
    p_in = lax.dot_general(q_in, act_ref[...], NT, preferred_element_type=jnp.float32)
    p_out = lax.dot_general(q_out, grad_ref[...], NT, preferred_element_type=jnp.float32)
    return p_in, p_out


def away_kernel(blocks, feat_ref, act_ref, grad_ref, *refs):
    out_ref = refs[blocks]
    p_in, p_out = project(act_ref, grad_ref, refs[:blocks])
    half = p_in.shape[0]
    out_ref[0, :half, :] = p_in
    out_ref[0, half:, :] = p_out


def home_kernel(blocks, cuts, feat_ref, act_ref, grad_ref, *refs):
    factors, got_ref, outs = refs[:blocks], refs[blocks], refs[blocks + 1 :]
    j = pl.program_id(0)
    p_in, p_out = project(act_ref, grad_ref, factors)
    total = jnp.concatenate([p_in, p_out], axis=0) + got_ref[0]
    for t, order in enumerate(ORDERS):
        send_ref, keep_ref = outs[2 * t], outs[2 * t + 1]
        part = total[cuts[t] : cuts[t + 1]]
        bits = [(j >> d) & 1 for d in order]
        pos = bits[1] * 2 + bits[2]

        @pl.when(bits[0] == 1)
        def _(send_ref=send_ref, part=part, pos=pos):
            put(send_ref, pos, part)

        @pl.when(bits[0] == 0)
        def _(keep_ref=keep_ref, part=part, pos=pos):
            keep_ref[pos] = part


def step_kernel(count, *refs):
    half = count // 2
    keeps, gots, outs = refs[:3], refs[3:6], refs[6:]
    for t in range(3):
        send_ref, keep_ref = outs[2 * t], outs[2 * t + 1]
        for pos in range(half):
            put(send_ref, pos, keeps[t][half + pos] + get(gots[t], half + pos))
        for pos in range(half):
            keep_ref[pos] = keeps[t][pos] + get(gots[t], pos)


def last_kernel(chunks, tok_ref, *refs):
    out_ref = refs[-1]
    tok = tok_ref[0]
    for c, owners in enumerate(chunks):
        keeps, gots = refs[6 * c : 6 * c + 3], refs[6 * c + 3 : 6 * c + 6]
        total = jnp.concatenate([k[0] + get(g, 0) for k, g in zip(keeps, gots)], axis=0)
        half = total.shape[0] // 2
        product = (total[:half] * total[half:]).reshape(half // RANK, RANK, BLOCK)
        score = jnp.sum(product, axis=1)
        per = score.shape[0] // len(owners)
        for i, (flip, turn) in enumerate(owners):
            owner = ((tok & 4) ^ flip) | ((tok + turn) & 3)
            for k in range(per):
                out_ref[pl.ds(owner * per + k, 1), :] = score[i * per + k : i * per + k + 1, :]


def params():
    return pltpu.CompilerParams(vmem_limit_bytes=VMEM)


def cuts_of(chunk_index, rows):
    groups = rows // RANK
    sizes = [groups // 3 + (1 if (i + chunk_index) % 3 < groups % 3 else 0) for i in range(3)]
    cuts = [0]
    for size in sizes:
        cuts.append(cuts[-1] + size * RANK)
    return cuts


def away(feat, acts, grads, factors):
    rows = 2 * sum(f.shape[0] for f in factors)
    k_in, k_out = acts.shape[1], grads.shape[1]
    spec = lambda k: pl.BlockSpec((BLOCK, k), lambda j, feat: (block_of(feat[0], j, 1), 0))
    fixed = [pl.BlockSpec(f.shape, lambda j, feat: (0, 0)) for f in factors]
    return pl.pallas_call(
        functools.partial(away_kernel, len(factors)),
        grid_spec=pltpu.PrefetchScalarGridSpec(
            num_scalar_prefetch=1,
            grid=(8,),
            in_specs=[spec(k_in), spec(k_out), *fixed],
            out_specs=pl.BlockSpec((1, rows, BLOCK), lambda j, feat: (j, 0, 0)),
        ),
        out_shape=jax.ShapeDtypeStruct((8, rows, BLOCK), jnp.float32),
        compiler_params=params(),
        cost_estimate=pl.CostEstimate(
            flops=8 * BLOCK * rows * (k_in + k_out), transcendentals=0,
            bytes_accessed=8 * BLOCK * (2 * (k_in + k_out) + 4 * rows)),
    )(feat, acts, grads, *factors)


def home(feat, acts, grads, factors, got, cuts):
    rows = got.shape[1]
    k_in, k_out = acts.shape[1], grads.shape[1]
    spec = lambda k: pl.BlockSpec((BLOCK, k), lambda j, feat: (block_of(feat[0], j, 0), 0))
    fixed = [pl.BlockSpec(f.shape, lambda j, feat: (0, 0)) for f in factors]
    shapes = []
    for t in range(3):
        n = cuts[t + 1] - cuts[t]
        shapes += [jax.ShapeDtypeStruct((4, n + 16, BLOCK), jnp.bfloat16),
                   jax.ShapeDtypeStruct((4, n, BLOCK), jnp.float32)]
    return pl.pallas_call(
        functools.partial(home_kernel, len(factors), cuts),
        grid_spec=pltpu.PrefetchScalarGridSpec(
            num_scalar_prefetch=1,
            grid=(8,),
            in_specs=[spec(k_in), spec(k_out), *fixed,
                      pl.BlockSpec((1, rows, BLOCK), lambda j, feat: (j, 0, 0))],
            out_specs=[pl.BlockSpec(s.shape, lambda j, feat: (0, 0, 0)) for s in shapes],
        ),
        out_shape=shapes,
        compiler_params=params(),
        cost_estimate=pl.CostEstimate(
            flops=8 * BLOCK * rows * (k_in + k_out), transcendentals=8 * BLOCK * rows,
            bytes_accessed=8 * BLOCK * (2 * (k_in + k_out) + 8 * rows)),
    )(feat, acts, grads, *factors, got)


def step(count, keeps, gots):
    half = count // 2
    shapes = []
    for keep in keeps:
        n = keep.shape[1]
        shapes += [jax.ShapeDtypeStruct((half, n + 16, BLOCK), jnp.bfloat16),
                   jax.ShapeDtypeStruct((half, n, BLOCK), jnp.float32)]
    rows = sum(k.shape[1] for k in keeps)
    return pl.pallas_call(
        functools.partial(step_kernel, count),
        out_shape=shapes,
        compiler_params=params(),
        cost_estimate=pl.CostEstimate(
            flops=count * rows * BLOCK * 20, transcendentals=2 * count * rows * BLOCK,
            bytes_accessed=count * rows * BLOCK * 10),
    )(*keeps, *gots)


def local(activations, out_grads, query_in, query_out):
    per, rank, k_in = query_in.shape
    feat = jnp.reshape(lax.axis_index("feat"), (1,)).astype(jnp.int32)
    tok = jnp.reshape(lax.axis_index("tok"), (1,)).astype(jnp.int32)
    up = [(s, (s & 4) | ((s + 1) & 3)) for s in range(8)]
    down = [(s, (s & 4) | ((s + 3) & 3)) for s in range(8)]
    across = [(s, s ^ 4) for s in range(8)]
    send_tok = lambda value, pairs: lax.ppermute(value, "tok", pairs)

    own = jnp.concatenate([query_in, query_out], axis=2).reshape(per * rank, -1)
    far = send_tok(own, across)
    own_up, own_down = send_tok(own, up), send_tok(own, down)
    far_up, far_down = send_tok(far, up), send_tok(far, down)
    own_two = send_tok(own_up, up)
    far_two = send_tok(far_down, down)
    chunks = [
        ((own, far), ((0, 0), (4, 0))),
        ((own_up, own_down), ((0, 3), (0, 1))),
        ((far_up, far_down), ((4, 3), (4, 1))),
        ((own_two, far_two), ((0, 2), (4, 2))),
    ]
    ends = []
    for c, (factors, _) in enumerate(chunks):
        rows = 2 * sum(f.shape[0] for f in factors)
        cuts = cuts_of(c, rows)
        got = send_feat(away(feat, activations, out_grads, factors), "core")
        outs = home(feat, activations, out_grads, factors, got, cuts)
        for stage, count in enumerate((4, 2)):
            gots = [send_feat(outs[2 * t], ORDERS[t][stage]) for t in range(3)]
            outs = step(count, outs[1::2], gots)
        gots = [send_feat(outs[2 * t], ORDERS[t][2]) for t in range(3)]
        ends += [*outs[1::2], *gots]
    total = per * lax.axis_size("tok")
    return pl.pallas_call(
        functools.partial(last_kernel, [owners for _, owners in chunks]),
        in_specs=[pl.BlockSpec(memory_space=pltpu.SMEM)] + [pl.BlockSpec(memory_space=pltpu.VMEM)] * len(ends),
        out_shape=jax.ShapeDtypeStruct((total, BLOCK), jnp.float32),
        compiler_params=params(),
    )(tok, *ends)


def solution(mesh):
    in_specs = (P("tok", "feat"), P("tok", "feat"), P("tok", None, "feat"), P("tok", None, "feat"))
    out_specs = P(None, ("tok", "feat"))
    return jax.shard_map(local, mesh=mesh, in_specs=in_specs, out_specs=out_specs, check_vma=False)
```

```python
import functools

import jax
import jax.numpy as jnp
from jax import lax
from jax.experimental import pallas as pl
from jax.experimental.pallas import tpu as pltpu
from jax.sharding import PartitionSpec as P

RANK = 32
BLOCK = 256
SPAN = 125.0
UNIT = (1.4426950408889634 / SPAN) ** 2
VMEM = 16 * 2**20
NT = (((1,), (1,)), ((), ()))
IN_VMEM = pl.BlockSpec(memory_space=pltpu.VMEM)
IN_SMEM = pl.BlockSpec(memory_space=pltpu.SMEM)

G1, G0, X = 2, 1, 0
ORDERS = (
    ((G0, X, G1), (G1, G0, X)),
    ((X, G1, G0), (G1, X, G0)),
    ((G0, X, G1), (X, G0, G1)),
)
CHUNKS = (
    ("own_up", "own_down", "own", "far"),
    ("own_two", "far_down", "far_up"),
    ("far_two",),
)
PLAN = (
    ("home", 0), ("away", 1), ("home", 1), ("step", 0, 1), ("away", 2), ("step", 0, 2), ("home", 2),
    ("step", 1, 1), ("step", 2, 1), ("step", 1, 2), ("step", 2, 2),
)
OWNERS = {
    "own": (0, 0), "far": (4, 0), "own_up": (0, 3), "own_down": (0, 1),
    "far_up": (4, 3), "far_down": (4, 1), "own_two": (0, 2), "far_two": (4, 2),
}


def gray(y):
    return y ^ (y >> 1)


def block_of(feat, orders, j, away):
    core = feat & 1
    spread = [sum(((j >> (2 - i)) & 1) << bit for i, bit in enumerate(order)) for order in orders]
    flips = spread[0] + (core ^ away) * (spread[1] - spread[0])
    y = gray(gray(feat >> 2) ^ (flips >> 1))
    return (y << 2) | ((((feat >> 1) & 1) ^ (flips & 1)) << 1) | (core ^ away)


def partner(device, bit):
    if bit == X:
        return device ^ 2
    flip = 1 if bit == G0 else 2
    return (gray(gray(device >> 2) ^ flip) << 2) | (device & 3)


def halve(value, orders, stage):
    return lax.ppermute(value, "feat", [(s, partner(s, orders[s & 1][stage])) for s in range(16)])


def put(ref, pos, value):
    rows, cols = value.shape
    grouped = value.reshape(rows // RANK, RANK, cols)
    top = jnp.max(jnp.abs(grouped), axis=1, keepdims=True)
    scale = (top * 1.01 + 1e-35).astype(jnp.bfloat16).astype(jnp.float32)
    part = grouped * (1.0 / scale)
    root = part * lax.rsqrt(jnp.abs(part) + 1e-30)
    ref[pos, :rows, :] = jnp.exp2(root * SPAN).reshape(rows, cols).astype(jnp.bfloat16)
    row = lax.broadcasted_iota(jnp.int32, (16, cols), 0)
    packed = jnp.zeros((16, cols), jnp.float32)
    for g in range(rows // RANK):
        packed = jnp.where(row == g, scale[g], packed)
    ref[pos, rows : rows + 16, :] = packed.astype(jnp.bfloat16)


def get(ref, pos):
    rows, cols = ref.shape[1] - 16, ref.shape[2]
    scale = ref[pos, rows : rows + 16, :].astype(jnp.float32)[: rows // RANK, :]
    root = jnp.log(ref[pos, :rows, :].astype(jnp.float32)).reshape(rows // RANK, RANK, cols)
    return (root * jnp.abs(root) * (scale * UNIT).reshape(rows // RANK, 1, cols)).reshape(rows, cols)


def gather_factors(factors, q_ref):
    row = 0
    for f in factors:
        q_ref[row : row + f.shape[0], :] = f[...]
        row += f.shape[0]


def project(act_ref, grad_ref, q_ref, block):
    n_in = act_ref.shape[1]
    rows = pl.ds(pl.multiple_of(block * BLOCK, BLOCK), BLOCK)
    p_in = lax.dot_general(q_ref[:, :n_in], act_ref[rows, :], NT, preferred_element_type=jnp.float32)
    p_out = lax.dot_general(q_ref[:, n_in:], grad_ref[rows, :], NT, preferred_element_type=jnp.float32)
    return p_in, p_out


def load_kernel(parts, act_ref, grad_ref, act_out, grad_out, sems):
    copies = []
    for src, dst in ((act_ref, act_out), (grad_ref, grad_out)):
        share = src.shape[0] // parts
        for i in range(parts):
            rows = pl.ds(i * share, share)
            copies.append(pltpu.make_async_copy(src.at[rows, :], dst.at[rows, :], sems.at[len(copies)]))
    for copy in copies:
        copy.start()
    for copy in copies:
        copy.wait()


def load(arrays):
    parts = 8
    return pl.pallas_call(
        functools.partial(load_kernel, parts),
        in_specs=[pl.BlockSpec(memory_space=pltpu.HBM)] * 2,
        out_specs=[IN_VMEM] * 2,
        out_shape=[pltpu.VMEM(x.shape, x.dtype) for x in arrays],
        scratch_shapes=[pltpu.SemaphoreType.DMA((2 * parts,))],
        compiler_params=pltpu.CompilerParams(vmem_limit_bytes=VMEM),
        cost_estimate=pl.CostEstimate(flops=0, transcendentals=0, bytes_accessed=sum(x.size * 2 for x in arrays)),
    )(*(pltpu.with_memory_space_constraint(x, pltpu.HBM) for x in arrays))


def away_kernel(blocks, orders, feat_ref, act_ref, grad_ref, *refs):
    out_ref, q_ref = refs[blocks:]
    gather_factors(refs[:blocks], q_ref)
    for j in range(8):
        p_in, p_out = project(act_ref, grad_ref, q_ref, block_of(feat_ref[0], orders, j, 1))
        put(out_ref, j, jnp.concatenate([p_in, p_out], axis=0))


def home_kernel(blocks, orders, feat_ref, act_ref, grad_ref, *refs):
    got_ref, send_ref, keep_ref, q_ref = refs[blocks:]
    gather_factors(refs[:blocks], q_ref)
    for j in (4, 5, 6, 7, 0, 1, 2, 3):
        p_in, p_out = project(act_ref, grad_ref, q_ref, block_of(feat_ref[0], orders, j, 0))
        total = jnp.concatenate([p_in, p_out], axis=0) + get(got_ref, j)
        if j >= 4:
            put(send_ref, j - 4, total)
        else:
            keep_ref[j] = total


def step_kernel(keep_ref, got_ref, send_ref, left_ref):
    half = left_ref.shape[0]
    for pos in range(half):
        put(send_ref, pos, keep_ref[half + pos] + get(got_ref, half + pos))
    for pos in range(half):
        left_ref[pos] = keep_ref[pos] + get(got_ref, pos)


def last_kernel(tok_ref, *refs):
    out_ref = refs[-1]
    tok = tok_ref[0]
    for c, names in enumerate(CHUNKS):
        keep_ref, got_ref = refs[2 * c : 2 * c + 2]
        total = keep_ref[0] + get(got_ref, 0)
        half = total.shape[0] // 2
        product = (total[:half] * total[half:]).reshape(half // RANK, RANK, BLOCK)
        score = jnp.sum(product, axis=1)
        per = score.shape[0] // len(names)
        for i, name in enumerate(names):
            flip, turn = OWNERS[name]
            owner = ((tok & 4) ^ flip) | ((tok + turn) & 3)
            for k in range(per):
                out_ref[pl.ds(owner * per + k, 1), :] = score[i * per + k : i * per + k + 1, :]


def call(kernel, shapes, operands, flops=0, transcendentals=0, scalars=1, scratch=(), after=None):
    moved = sum(o.size * o.dtype.itemsize for o in operands)
    specs = [IN_SMEM] * scalars + [IN_VMEM] * (len(operands) - scalars)
    if after is not None:
        inner, place = kernel, len(operands)
        kernel = lambda *refs: inner(*refs[:place], *refs[place + 1 :])
        operands, specs = (*operands, after), [*specs, pl.BlockSpec(memory_space=pl.ANY)]
    return pl.pallas_call(
        kernel,
        in_specs=specs,
        out_specs=jax.tree.map(lambda _: IN_VMEM, shapes),
        out_shape=shapes,
        scratch_shapes=scratch,
        compiler_params=pltpu.CompilerParams(vmem_limit_bytes=VMEM),
        cost_estimate=pl.CostEstimate(flops=flops, transcendentals=transcendentals, bytes_accessed=moved),
    )(*operands)


def sends(count, rows):
    return [jax.ShapeDtypeStruct((count, rows + 16, BLOCK), jnp.bfloat16),
            jax.ShapeDtypeStruct((count, rows, BLOCK), jnp.float32)]


def local(activations, out_grads, query_in, query_out):
    per, rank, k_in = query_in.shape
    feat = jnp.reshape(lax.axis_index("feat"), (1,)).astype(jnp.int32)
    tok = jnp.reshape(lax.axis_index("tok"), (1,)).astype(jnp.int32)
    pairs = {
        "up": [(s, (s & 4) | ((s + 1) & 3)) for s in range(8)],
        "down": [(s, (s & 4) | ((s + 3) & 3)) for s in range(8)],
        "across": [(s, s ^ 4) for s in range(8)],
    }
    move = lambda value, way: lax.ppermute(value, "tok", pairs[way])

    own = jnp.concatenate([query_in, query_out], axis=2).reshape(per * rank, -1)
    factor = {"own": own, "own_up": move(own, "up"), "own_down": move(own, "down"), "far": move(own, "across")}
    acts, grads = load((activations, out_grads))
    turn = {"after": None}
    got, keep = {}, {}

    def away(c):
        blocks = [factor[name] for name in CHUNKS[c]]
        side, width = sum(b.shape[0] for b in blocks), own.shape[1]
        scratch = [pltpu.VMEM((side, width), jnp.bfloat16)]
        send = call(functools.partial(away_kernel, len(blocks), ORDERS[c]), sends(8, 2 * side)[0],
                    (feat, acts, grads, *blocks), 2 * 8 * BLOCK * side * width, 0, 1, scratch, **turn)
        turn["after"] = send
        got[c] = lax.ppermute(send, "feat", [(s, s ^ 1) for s in range(16)])

    def home(c):
        blocks = [factor[name] for name in CHUNKS[c]]
        side, width = sum(b.shape[0] for b in blocks), own.shape[1]
        scratch = [pltpu.VMEM((side, width), jnp.bfloat16)]
        send, keep[c] = call(functools.partial(home_kernel, len(blocks), ORDERS[c]), sends(4, 2 * side),
                             (feat, acts, grads, *blocks, got[c]), 2 * 8 * BLOCK * side * width, 0, 1, scratch, **turn)
        turn["after"] = send
        got[c] = halve(send, ORDERS[c], 0)

    def step(c, stage):
        count, rows = keep[c].shape[:2]
        send, keep[c] = call(step_kernel, sends(count // 2, rows), (keep[c], got[c]),
                             20 * count * rows * BLOCK, 0, 0, **turn)
        turn["after"] = send
        got[c] = halve(send, ORDERS[c], stage)

    away(0)
    own_up, far, _ = lax.optimization_barrier((factor["own_up"], factor["far"], turn["after"]))
    factor["own_two"] = move(own_up, "up")
    factor["far_down"] = move(far, "down")
    factor["far_up"] = move(own_up, "across")
    factor["far_two"] = move(factor["own_two"], "across")
    for item in PLAN:
        kind, c = item[0], item[1]
        if kind == "away":
            away(c)
        elif kind == "home":
            home(c)
        else:
            step(c, item[2])
    ends = [x for c in range(len(CHUNKS)) for x in (keep[c], got[c])]
    return call(last_kernel, jax.ShapeDtypeStruct((per * lax.axis_size("tok"), BLOCK), jnp.float32), (tok, *ends))


def solution(mesh):
    in_specs = (P("tok", "feat"), P("tok", "feat"), P("tok", None, "feat"), P("tok", None, "feat"))
    out_specs = P(None, ("tok", "feat"))
    return jax.shard_map(local, mesh=mesh, in_specs=in_specs, out_specs=out_specs, check_vma=False)
```

```python
import functools

import jax
import jax.numpy as jnp
from jax import lax
from jax.experimental import pallas as pl
from jax.experimental.pallas import tpu as pltpu
from jax.sharding import PartitionSpec as P

RANK = 32
BLOCK = 256
SPAN = 125.0
UNIT = (1.4426950408889634 / SPAN) ** 2
VMEM = 16 * 2**20
NT = (((1,), (1,)), ((), ()))
IN_VMEM = pl.BlockSpec(memory_space=pltpu.VMEM)
IN_SMEM = pl.BlockSpec(memory_space=pltpu.SMEM)

G1, G0, X = 2, 1, 0
ORDERS = (
    ((G0, G1, X), (G1, X, G0)),
    ((X, G0, G1), (G0, G1, X)),
    ((X, G1, G0), (G1, X, G0)),
)
CHUNKS = (
    ("own_up", "own_down", "own", "far"),
    ("own_two", "far_down", "far_up"),
    ("far_two",),
)
COST = 1024
PLAN = (
    ("away", 0), ("home", 0), ("pass", 2), ("away", 1), ("home", 1), ("away", 2), ("step", 0, 1), ("home", 2),
    ("step", 1, 1), ("step", 0, 2), ("step", 2, 1), ("step", 1, 2), ("step", 2, 2),
)
OWNERS = {
    "own": (0, 0), "far": (4, 0), "own_up": (0, 3), "own_down": (0, 1),
    "far_up": (4, 3), "far_down": (4, 1), "own_two": (0, 2), "far_two": (4, 2),
}


def gray(y):
    return y ^ (y >> 1)


def block_of(feat, orders, j, away):
    core = feat & 1
    spread = [sum(((j >> (2 - i)) & 1) << bit for i, bit in enumerate(order)) for order in orders]
    flips = spread[0] + (core ^ away) * (spread[1] - spread[0])
    y = gray(gray(feat >> 2) ^ (flips >> 1))
    return (y << 2) | ((((feat >> 1) & 1) ^ (flips & 1)) << 1) | (core ^ away)


def partner(device, bit):
    if bit == X:
        return device ^ 2
    flip = 1 if bit == G0 else 2
    return (gray(gray(device >> 2) ^ flip) << 2) | (device & 3)


def halve(value, orders, stage):
    return lax.ppermute(value, "feat", [(s, partner(s, orders[s & 1][stage])) for s in range(16)])


def put(ref, pos, value):
    rows, cols = value.shape
    grouped = value.reshape(rows // RANK, RANK, cols)
    top = jnp.max(jnp.abs(grouped), axis=1, keepdims=True)
    scale = (top * 1.01 + 1e-35).astype(jnp.bfloat16).astype(jnp.float32)
    part = grouped * (1.0 / scale)
    root = part * lax.rsqrt(jnp.abs(part) + 1e-30)
    ref[pos, :rows, :] = jnp.exp2(root * SPAN).reshape(rows, cols).astype(jnp.bfloat16)
    row = lax.broadcasted_iota(jnp.int32, (16, cols), 0)
    packed = jnp.zeros((16, cols), jnp.float32)
    for g in range(rows // RANK):
        packed = jnp.where(row == g, scale[g], packed)
    ref[pos, rows : rows + 16, :] = packed.astype(jnp.bfloat16)


def get(ref, pos):
    rows, cols = ref.shape[1] - 16, ref.shape[2]
    scale = ref[pos, rows : rows + 16, :].astype(jnp.float32)[: rows // RANK, :]
    root = jnp.log(ref[pos, :rows, :].astype(jnp.float32)).reshape(rows // RANK, RANK, cols)
    return (root * jnp.abs(root) * (scale * UNIT).reshape(rows // RANK, 1, cols)).reshape(rows, cols)


def gather_factors(factors, q_ref):
    row = 0
    for f in factors:
        q_ref[row : row + f.shape[0], :] = f[...]
        row += f.shape[0]


def project(act_ref, grad_ref, q_ref, block):
    n_in = act_ref.shape[1]
    rows = pl.ds(pl.multiple_of(block * BLOCK, BLOCK), BLOCK)
    p_in = lax.dot_general(q_ref[:, :n_in], act_ref[rows, :], NT, preferred_element_type=jnp.float32)
    p_out = lax.dot_general(q_ref[:, n_in:], grad_ref[rows, :], NT, preferred_element_type=jnp.float32)
    return p_in, p_out


def load_kernel(parts, act_ref, grad_ref, act_out, grad_out, sems):
    copies = []
    for src, dst in ((act_ref, act_out), (grad_ref, grad_out)):
        share = src.shape[0] // parts
        for i in range(parts):
            rows = pl.ds(i * share, share)
            copies.append(pltpu.make_async_copy(src.at[rows, :], dst.at[rows, :], sems.at[len(copies)]))
    for copy in copies:
        copy.start()
    for copy in copies:
        copy.wait()


def load(arrays):
    parts = 8
    return pl.pallas_call(
        functools.partial(load_kernel, parts),
        in_specs=[pl.BlockSpec(memory_space=pltpu.HBM)] * 2,
        out_specs=[IN_VMEM] * 2,
        out_shape=[pltpu.VMEM(x.shape, x.dtype) for x in arrays],
        scratch_shapes=[pltpu.SemaphoreType.DMA((2 * parts,))],
        compiler_params=pltpu.CompilerParams(vmem_limit_bytes=VMEM),
        cost_estimate=pl.CostEstimate(flops=0, transcendentals=0, bytes_accessed=sum(x.size * 2 for x in arrays)),
    )(*(pltpu.with_memory_space_constraint(x, pltpu.HBM) for x in arrays))


def away_kernel(blocks, orders, feat_ref, act_ref, grad_ref, *refs):
    out_ref, q_ref = refs[blocks:]
    gather_factors(refs[:blocks], q_ref)
    for j in range(8):
        p_in, p_out = project(act_ref, grad_ref, q_ref, block_of(feat_ref[0], orders, j, 1))
        put(out_ref, j, jnp.concatenate([p_in, p_out], axis=0))


def home_kernel(blocks, orders, feat_ref, act_ref, grad_ref, *refs):
    got_ref, send_ref, keep_ref, q_ref = refs[blocks:]
    gather_factors(refs[:blocks], q_ref)
    for j in (4, 5, 6, 7, 0, 1, 2, 3):
        p_in, p_out = project(act_ref, grad_ref, q_ref, block_of(feat_ref[0], orders, j, 0))
        total = jnp.concatenate([p_in, p_out], axis=0) + get(got_ref, j)
        if j >= 4:
            put(send_ref, j - 4, total)
        else:
            keep_ref[j] = total


def step_kernel(keep_ref, got_ref, send_ref, left_ref):
    half = left_ref.shape[0]
    for pos in range(half):
        put(send_ref, pos, keep_ref[half + pos] + get(got_ref, half + pos))
    for pos in range(half):
        left_ref[pos] = keep_ref[pos] + get(got_ref, pos)


def last_kernel(tok_ref, *refs):
    out_ref = refs[-1]
    tok = tok_ref[0]
    for c, names in enumerate(CHUNKS):
        keep_ref, got_ref = refs[2 * c : 2 * c + 2]
        total = keep_ref[0] + get(got_ref, 0)
        half = total.shape[0] // 2
        product = (total[:half] * total[half:]).reshape(half // RANK, RANK, BLOCK)
        score = jnp.sum(product, axis=1)
        per = score.shape[0] // len(names)
        for i, name in enumerate(names):
            flip, turn = OWNERS[name]
            owner = ((tok & 4) ^ flip) | ((tok + turn) & 3)
            for k in range(per):
                out_ref[pl.ds(owner * per + k, 1), :] = score[i * per + k : i * per + k + 1, :]


def call(kernel, shapes, operands, flops=0, transcendentals=0, scalars=1, scratch=(), after=None, name=None):
    moved = sum(o.size * o.dtype.itemsize for o in operands)
    specs = [IN_SMEM] * scalars + [IN_VMEM] * (len(operands) - scalars)
    if after is not None:
        inner, place = kernel, len(operands)
        kernel = lambda *refs: inner(*refs[:place], *refs[place + 1 :])
        operands, specs = (*operands, after), [*specs, pl.BlockSpec(memory_space=pl.ANY)]
    return pl.pallas_call(
        kernel,
        in_specs=specs,
        out_specs=jax.tree.map(lambda _: IN_VMEM, shapes),
        out_shape=shapes,
        scratch_shapes=scratch,
        name=name,
        compiler_params=pltpu.CompilerParams(vmem_limit_bytes=VMEM),
        cost_estimate=pl.CostEstimate(flops=flops, transcendentals=0, bytes_accessed=1024),
    )(*operands)


def sends(count, rows):
    return [jax.ShapeDtypeStruct((count, rows + 16, BLOCK), jnp.bfloat16),
            jax.ShapeDtypeStruct((count, rows, BLOCK), jnp.float32)]


def local(activations, out_grads, query_in, query_out):
    per, rank, k_in = query_in.shape
    feat = jnp.reshape(lax.axis_index("feat"), (1,)).astype(jnp.int32)
    tok = jnp.reshape(lax.axis_index("tok"), (1,)).astype(jnp.int32)
    pairs = {
        "up": [(s, (s & 4) | ((s + 1) & 3)) for s in range(8)],
        "down": [(s, (s & 4) | ((s + 3) & 3)) for s in range(8)],
        "across": [(s, s ^ 4) for s in range(8)],
    }
    move = lambda value, way: lax.ppermute(value, "tok", pairs[way])

    own = jnp.concatenate([query_in, query_out], axis=2).reshape(per * rank, -1)
    factor = {"own": own, "own_up": move(own, "up"), "own_down": move(own, "down"), "far": move(own, "across")}
    acts, grads = load((activations, out_grads))
    turn = {"after": None}
    got, keep = {}, {}

    def away(c):
        blocks = [factor[name] for name in CHUNKS[c]]
        side, width = sum(b.shape[0] for b in blocks), own.shape[1]
        scratch = [pltpu.VMEM((side, width), jnp.bfloat16)]
        send = call(functools.partial(away_kernel, len(blocks), ORDERS[c]), sends(8, 2 * side)[0],
                    (feat, acts, grads, *blocks), 1024, 0, 1, scratch, name=f"away_{c}", **turn)
        turn["after"] = send
        got[c] = lax.ppermute(send, "feat", [(s, s ^ 1) for s in range(16)])

    def home(c):
        blocks = [factor[name] for name in CHUNKS[c]]
        side, width = sum(b.shape[0] for b in blocks), own.shape[1]
        scratch = [pltpu.VMEM((side, width), jnp.bfloat16)]
        send, keep[c] = call(functools.partial(home_kernel, len(blocks), ORDERS[c]), sends(4, 2 * side),
                             (feat, acts, grads, *blocks, got[c]), 1024, 0, 1, scratch, name=f"home_{c}", **turn)
        turn["after"] = send
        got[c] = halve(send, ORDERS[c], 0)

    def step(c, stage):
        count, rows = keep[c].shape[:2]
        send, keep[c] = call(step_kernel, sends(count // 2, rows), (keep[c], got[c]),
                             COST, 0, 0, name=f"step_{c}_{stage}", **turn)
        turn["after"] = send
        got[c] = halve(send, ORDERS[c], stage)

    factor["own_two"] = move(factor["own_up"], "up")
    factor["far_down"] = move(factor["far"], "down")
    factor["far_up"] = move(factor["own_up"], "across")
    for item in PLAN:
        kind, c = item[0], item[1]
        if kind == "away":
            away(c)
        elif kind == "home":
            home(c)
        elif kind == "pass":
            ahead, _ = lax.optimization_barrier((factor["own_two"], turn["after"]))
            factor["far_two"] = move(ahead, "across")
        else:
            step(c, item[2])
    ends = [x for c in range(len(CHUNKS)) for x in (keep[c], got[c])]
    return call(last_kernel, jax.ShapeDtypeStruct((per * lax.axis_size("tok"), BLOCK), jnp.float32), (tok, *ends))


def solution(mesh):
    in_specs = (P("tok", "feat"), P("tok", "feat"), P("tok", None, "feat"), P("tok", None, "feat"))
    out_specs = P(None, ("tok", "feat"))
    return jax.shard_map(local, mesh=mesh, in_specs=in_specs, out_specs=out_specs, check_vma=False)
```

```python
import functools

import jax
import jax.numpy as jnp
from jax import lax
from jax.experimental import pallas as pl
from jax.experimental.pallas import tpu as pltpu
from jax.sharding import PartitionSpec as P

RANK = 32
BLOCK = 256
SPAN = 125.0
UNIT = (1.4426950408889634 / SPAN) ** 2
VMEM = 16 * 2**20
NT = (((1,), (1,)), ((), ()))
IN_VMEM = pl.BlockSpec(memory_space=pltpu.VMEM)
IN_SMEM = pl.BlockSpec(memory_space=pltpu.SMEM)

G1, G0, X = 2, 1, 0
ORDERS = (
    ((G0, X, G1), (G1, G0, X)),
    ((X, G1, G0), (G1, X, G0)),
    ((G0, G1, X), (X, G0, G1)),
)
CHUNKS = (
    ("own_up", "own_down", "own", "far"),
    ("own_two", "far_down", "far_up"),
    ("far_two",),
)
COST_OF = {}
PLAN = (
    ("away", 0), ("home", 0), ("pass", 2), ("away", 1), ("home", 1), ("away", 2), ("step", 0, 1),
    ("home", 2), ("step", 1, 1), ("step", 0, 2), ("step", 2, 1), ("step", 1, 2), ("step", 2, 2),
)
OWNERS = {
    "own": (0, 0), "far": (4, 0), "own_up": (0, 3), "own_down": (0, 1),
    "far_up": (4, 3), "far_down": (4, 1), "own_two": (0, 2), "far_two": (4, 2),
}


def gray(y):
    return y ^ (y >> 1)


def block_of(feat, orders, j, away):
    core = feat & 1
    spread = [sum(((j >> (2 - i)) & 1) << bit for i, bit in enumerate(order)) for order in orders]
    flips = spread[0] + (core ^ away) * (spread[1] - spread[0])
    y = gray(gray(feat >> 2) ^ (flips >> 1))
    return (y << 2) | ((((feat >> 1) & 1) ^ (flips & 1)) << 1) | (core ^ away)


def partner(device, bit):
    if bit == X:
        return device ^ 2
    flip = 1 if bit == G0 else 2
    return (gray(gray(device >> 2) ^ flip) << 2) | (device & 3)


def halve(value, orders, stage):
    return lax.ppermute(value, "feat", [(s, partner(s, orders[s & 1][stage])) for s in range(16)])


def put(ref, pos, value):
    rows, cols = value.shape
    grouped = value.reshape(rows // RANK, RANK, cols)
    top = jnp.max(jnp.abs(grouped), axis=1, keepdims=True)
    scale = (top * 1.01 + 1e-35).astype(jnp.bfloat16).astype(jnp.float32)
    part = grouped * (1.0 / scale)
    root = part * lax.rsqrt(jnp.abs(part) + 1e-30)
    ref[pos, :rows, :] = jnp.exp2(root * SPAN).reshape(rows, cols).astype(jnp.bfloat16)
    row = lax.broadcasted_iota(jnp.int32, (16, cols), 0)
    packed = jnp.zeros((16, cols), jnp.float32)
    for g in range(rows // RANK):
        packed = jnp.where(row == g, scale[g], packed)
    ref[pos, rows : rows + 16, :] = packed.astype(jnp.bfloat16)


def get(ref, pos):
    rows, cols = ref.shape[1] - 16, ref.shape[2]
    scale = ref[pos, rows : rows + 16, :].astype(jnp.float32)[: rows // RANK, :]
    root = jnp.log(ref[pos, :rows, :].astype(jnp.float32)).reshape(rows // RANK, RANK, cols)
    return (root * jnp.abs(root) * (scale * UNIT).reshape(rows // RANK, 1, cols)).reshape(rows, cols)


def gather_factors(factors, q_ref):
    row = 0
    for f in factors:
        q_ref[row : row + f.shape[0], :] = f[...]
        row += f.shape[0]


def project(act_ref, grad_ref, q_ref, block):
    n_in = act_ref.shape[1]
    rows = pl.ds(pl.multiple_of(block * BLOCK, BLOCK), BLOCK)
    p_in = lax.dot_general(q_ref[:, :n_in], act_ref[rows, :], NT, preferred_element_type=jnp.float32)
    p_out = lax.dot_general(q_ref[:, n_in:], grad_ref[rows, :], NT, preferred_element_type=jnp.float32)
    return p_in, p_out


def load_kernel(parts, act_ref, grad_ref, act_out, grad_out, sems):
    copies = []
    for src, dst in ((act_ref, act_out), (grad_ref, grad_out)):
        share = src.shape[0] // parts
        for i in range(parts):
            rows = pl.ds(i * share, share)
            copies.append(pltpu.make_async_copy(src.at[rows, :], dst.at[rows, :], sems.at[len(copies)]))
    for copy in copies:
        copy.start()
    for copy in copies:
        copy.wait()


def load(arrays):
    parts = 8
    return pl.pallas_call(
        functools.partial(load_kernel, parts),
        in_specs=[pl.BlockSpec(memory_space=pltpu.HBM)] * 2,
        out_specs=[IN_VMEM] * 2,
        out_shape=[pltpu.VMEM(x.shape, x.dtype) for x in arrays],
        scratch_shapes=[pltpu.SemaphoreType.DMA((2 * parts,))],
        compiler_params=pltpu.CompilerParams(vmem_limit_bytes=VMEM),
        cost_estimate=pl.CostEstimate(flops=0, transcendentals=0, bytes_accessed=sum(x.size * 2 for x in arrays)),
    )(*(pltpu.with_memory_space_constraint(x, pltpu.HBM) for x in arrays))


def away_kernel(blocks, orders, feat_ref, act_ref, grad_ref, *refs):
    out_ref, q_ref = refs[blocks:]
    gather_factors(refs[:blocks], q_ref)
    for j in range(8):
        p_in, p_out = project(act_ref, grad_ref, q_ref, block_of(feat_ref[0], orders, j, 1))
        put(out_ref, j, jnp.concatenate([p_in, p_out], axis=0))


def home_kernel(blocks, orders, feat_ref, act_ref, grad_ref, *refs):
    got_ref, send_ref, keep_ref, q_ref = refs[blocks:]
    gather_factors(refs[:blocks], q_ref)
    for j in (4, 5, 6, 7, 0, 1, 2, 3):
        p_in, p_out = project(act_ref, grad_ref, q_ref, block_of(feat_ref[0], orders, j, 0))
        total = jnp.concatenate([p_in, p_out], axis=0) + get(got_ref, j)
        if j >= 4:
            put(send_ref, j - 4, total)
        else:
            keep_ref[j] = total


def step_kernel(keep_ref, got_ref, send_ref, left_ref):
    half = left_ref.shape[0]
    for pos in range(half):
        put(send_ref, pos, keep_ref[half + pos] + get(got_ref, half + pos))
    for pos in range(half):
        left_ref[pos] = keep_ref[pos] + get(got_ref, pos)


def last_kernel(tok_ref, *refs):
    out_ref = refs[-1]
    tok = tok_ref[0]
    for c, names in enumerate(CHUNKS):
        keep_ref, got_ref = refs[2 * c : 2 * c + 2]
        total = keep_ref[0] + get(got_ref, 0)
        half = total.shape[0] // 2
        product = (total[:half] * total[half:]).reshape(half // RANK, RANK, BLOCK)
        score = jnp.sum(product, axis=1)
        per = score.shape[0] // len(names)
        for i, name in enumerate(names):
            flip, turn = OWNERS[name]
            owner = ((tok & 4) ^ flip) | ((tok + turn) & 3)
            for k in range(per):
                out_ref[pl.ds(owner * per + k, 1), :] = score[i * per + k : i * per + k + 1, :]


def call(kernel, shapes, operands, flops=0, transcendentals=0, scalars=1, scratch=(), after=None, name=None):
    moved = sum(o.size * o.dtype.itemsize for o in operands)
    specs = [IN_SMEM] * scalars + [IN_VMEM] * (len(operands) - scalars)
    if after is not None:
        inner, place = kernel, len(operands)
        kernel = lambda *refs: inner(*refs[:place], *refs[place + 1 :])
        operands, specs = (*operands, after), [*specs, pl.BlockSpec(memory_space=pl.ANY)]
    return pl.pallas_call(
        kernel,
        in_specs=specs,
        out_specs=jax.tree.map(lambda _: IN_VMEM, shapes),
        out_shape=shapes,
        scratch_shapes=scratch,
        name=name,
        compiler_params=pltpu.CompilerParams(vmem_limit_bytes=VMEM),
        cost_estimate=pl.CostEstimate(flops=flops, transcendentals=0, bytes_accessed=1024),
    )(*operands)


def sends(count, rows):
    return [jax.ShapeDtypeStruct((count, rows + 16, BLOCK), jnp.bfloat16),
            jax.ShapeDtypeStruct((count, rows, BLOCK), jnp.float32)]


def local(activations, out_grads, query_in, query_out):
    per, rank, k_in = query_in.shape
    feat = jnp.reshape(lax.axis_index("feat"), (1,)).astype(jnp.int32)
    tok = jnp.reshape(lax.axis_index("tok"), (1,)).astype(jnp.int32)
    pairs = {
        "up": [(s, (s & 4) | ((s + 1) & 3)) for s in range(8)],
        "down": [(s, (s & 4) | ((s + 3) & 3)) for s in range(8)],
        "across": [(s, s ^ 4) for s in range(8)],
    }
    move = lambda value, way: lax.ppermute(value, "tok", pairs[way])

    own = jnp.concatenate([query_in, query_out], axis=2).reshape(per * rank, -1)
    factor = {"own": own, "own_up": move(own, "up"), "own_down": move(own, "down"), "far": move(own, "across")}
    acts, grads = load((activations, out_grads))
    turn = {"after": None}
    got, keep = {}, {}

    def away(c):
        blocks = [factor[name] for name in CHUNKS[c]]
        side, width = sum(b.shape[0] for b in blocks), own.shape[1]
        scratch = [pltpu.VMEM((side, width), jnp.bfloat16)]
        send = call(functools.partial(away_kernel, len(blocks), ORDERS[c]), sends(8, 2 * side)[0],
                    (feat, acts, grads, *blocks), COST_OF.get(f"away_{c}", 1024), 0, 1, scratch, name=f"away_{c}", **turn)
        turn["after"] = send
        got[c] = lax.ppermute(send, "feat", [(s, s ^ 1) for s in range(16)])

    def home(c):
        blocks = [factor[name] for name in CHUNKS[c]]
        side, width = sum(b.shape[0] for b in blocks), own.shape[1]
        scratch = [pltpu.VMEM((side, width), jnp.bfloat16)]
        send, keep[c] = call(functools.partial(home_kernel, len(blocks), ORDERS[c]), sends(4, 2 * side),
                             (feat, acts, grads, *blocks, got[c]), COST_OF.get(f"home_{c}", 1024), 0, 1, scratch, name=f"home_{c}", **turn)
        turn["after"] = send
        got[c] = halve(send, ORDERS[c], 0)

    def step(c, stage):
        count, rows = keep[c].shape[:2]
        send, keep[c] = call(step_kernel, sends(count // 2, rows), (keep[c], got[c]),
                             COST_OF.get(f"step_{c}_{stage}", 1024), 0, 0, name=f"step_{c}_{stage}", **turn)
        turn["after"] = send
        got[c] = halve(send, ORDERS[c], stage)

    factor["own_two"] = move(factor["own_up"], "up")
    factor["far_down"] = move(factor["far"], "down")
    factor["far_up"] = move(factor["own_up"], "across")
    for item in PLAN:
        kind, c = item[0], item[1]
        if kind == "away":
            away(c)
        elif kind == "home":
            home(c)
        elif kind == "pass":
            ahead, _ = lax.optimization_barrier((factor["own_two"], turn["after"]))
            factor["far_two"] = move(ahead, "across")
        else:
            step(c, item[2])
    ends = [x for c in range(len(CHUNKS)) for x in (keep[c], got[c])]
    return call(last_kernel, jax.ShapeDtypeStruct((per * lax.axis_size("tok"), BLOCK), jnp.float32), (tok, *ends))


def solution(mesh):
    in_specs = (P("tok", "feat"), P("tok", "feat"), P("tok", None, "feat"), P("tok", None, "feat"))
    out_specs = P(None, ("tok", "feat"))
    return jax.shard_map(local, mesh=mesh, in_specs=in_specs, out_specs=out_specs, check_vma=False)
```

```python
import functools

import jax
import jax.numpy as jnp
from jax import lax
from jax.experimental import pallas as pl
from jax.experimental.pallas import tpu as pltpu
from jax.sharding import PartitionSpec as P

RANK = 32
BLOCK = 256
SPAN = 125.0
UNIT = (1.4426950408889634 / SPAN) ** 2
VMEM = 16 * 2**20
NT = (((1,), (1,)), ((), ()))
IN_VMEM = pl.BlockSpec(memory_space=pltpu.VMEM)
IN_SMEM = pl.BlockSpec(memory_space=pltpu.SMEM)

G1, G0, X = 2, 1, 0
ORDERS = (
    ((G0, X, G1), (G1, G0, X)),
    ((X, G1, G0), (G1, X, G0)),
    ((G0, G1, X), (X, G0, G1)),
)
CHUNKS = (
    ("own_up", "own_down", "own", "far"),
    ("own_two", "far_down", "far_up"),
    ("far_two",),
)
COST_OF = {'step_1_1': 10000000000}
PLAN = (
    ("away", 0), ("home", 0), ("pass", 2), ("away", 1), ("home", 1), ("away", 2), ("step", 0, 1),
    ("home", 2), ("step", 1, 1), ("step", 0, 2), ("step", 2, 1), ("step", 1, 2), ("step", 2, 2),
)
OWNERS = {
    "own": (0, 0), "far": (4, 0), "own_up": (0, 3), "own_down": (0, 1),
    "far_up": (4, 3), "far_down": (4, 1), "own_two": (0, 2), "far_two": (4, 2),
}


def gray(y):
    return y ^ (y >> 1)


def block_of(feat, orders, j, away):
    core = feat & 1
    spread = [sum(((j >> (2 - i)) & 1) << bit for i, bit in enumerate(order)) for order in orders]
    flips = spread[0] + (core ^ away) * (spread[1] - spread[0])
    y = gray(gray(feat >> 2) ^ (flips >> 1))
    return (y << 2) | ((((feat >> 1) & 1) ^ (flips & 1)) << 1) | (core ^ away)


def partner(device, bit):
    if bit == X:
        return device ^ 2
    flip = 1 if bit == G0 else 2
    return (gray(gray(device >> 2) ^ flip) << 2) | (device & 3)


def halve(value, orders, stage):
    return lax.ppermute(value, "feat", [(s, partner(s, orders[s & 1][stage])) for s in range(16)])


def put(ref, pos, value):
    rows, cols = value.shape
    grouped = value.reshape(rows // RANK, RANK, cols)
    top = jnp.max(jnp.abs(grouped), axis=1, keepdims=True)
    scale = (top * 1.01 + 1e-35).astype(jnp.bfloat16).astype(jnp.float32)
    part = grouped * (1.0 / scale)
    root = part * lax.rsqrt(jnp.abs(part) + 1e-30)
    ref[pos, :rows, :] = jnp.exp2(root * SPAN).reshape(rows, cols).astype(jnp.bfloat16)
    row = lax.broadcasted_iota(jnp.int32, (16, cols), 0)
    packed = jnp.zeros((16, cols), jnp.float32)
    for g in range(rows // RANK):
        packed = jnp.where(row == g, scale[g], packed)
    ref[pos, rows : rows + 16, :] = packed.astype(jnp.bfloat16)


def get(ref, pos):
    rows, cols = ref.shape[1] - 16, ref.shape[2]
    scale = ref[pos, rows : rows + 16, :].astype(jnp.float32)[: rows // RANK, :]
    root = jnp.log(ref[pos, :rows, :].astype(jnp.float32)).reshape(rows // RANK, RANK, cols)
    return (root * jnp.abs(root) * (scale * UNIT).reshape(rows // RANK, 1, cols)).reshape(rows, cols)


def gather_factors(factors, q_ref):
    row = 0
    for f in factors:
        q_ref[row : row + f.shape[0], :] = f[...]
        row += f.shape[0]


def project(act_ref, grad_ref, q_ref, block):
    n_in = act_ref.shape[1]
    rows = pl.ds(pl.multiple_of(block * BLOCK, BLOCK), BLOCK)
    p_in = lax.dot_general(q_ref[:, :n_in], act_ref[rows, :], NT, preferred_element_type=jnp.float32)
    p_out = lax.dot_general(q_ref[:, n_in:], grad_ref[rows, :], NT, preferred_element_type=jnp.float32)
    return p_in, p_out


def load_kernel(parts, act_ref, grad_ref, act_out, grad_out, sems):
    copies = []
    for src, dst in ((act_ref, act_out), (grad_ref, grad_out)):
        share = src.shape[0] // parts
        for i in range(parts):
            rows = pl.ds(i * share, share)
            copies.append(pltpu.make_async_copy(src.at[rows, :], dst.at[rows, :], sems.at[len(copies)]))
    for copy in copies:
        copy.start()
    for copy in copies:
        copy.wait()


def load(arrays):
    parts = 8
    return pl.pallas_call(
        functools.partial(load_kernel, parts),
        in_specs=[pl.BlockSpec(memory_space=pltpu.HBM)] * 2,
        out_specs=[IN_VMEM] * 2,
        out_shape=[pltpu.VMEM(x.shape, x.dtype) for x in arrays],
        scratch_shapes=[pltpu.SemaphoreType.DMA((2 * parts,))],
        compiler_params=pltpu.CompilerParams(vmem_limit_bytes=VMEM),
        cost_estimate=pl.CostEstimate(flops=0, transcendentals=0, bytes_accessed=sum(x.size * 2 for x in arrays)),
    )(*(pltpu.with_memory_space_constraint(x, pltpu.HBM) for x in arrays))


def pack_kernel(in_ref, out_ref, own_ref, sems):
    n_in = in_ref.shape[1]
    first = pltpu.make_async_copy(in_ref, own_ref.at[:, :n_in], sems.at[0])
    second = pltpu.make_async_copy(out_ref, own_ref.at[:, n_in:], sems.at[1])
    first.start()
    second.start()
    first.wait()
    second.wait()


def pack(q_in, q_out):
    return pl.pallas_call(
        pack_kernel,
        in_specs=[pl.BlockSpec(memory_space=pltpu.HBM)] * 2,
        out_specs=IN_VMEM,
        out_shape=pltpu.VMEM((q_in.shape[0], q_in.shape[1] + q_out.shape[1]), q_in.dtype),
        scratch_shapes=[pltpu.SemaphoreType.DMA((2,))],
        compiler_params=pltpu.CompilerParams(vmem_limit_bytes=VMEM),
        cost_estimate=pl.CostEstimate(flops=0, transcendentals=0, bytes_accessed=1024),
    )(*(pltpu.with_memory_space_constraint(x, pltpu.HBM) for x in (q_in, q_out)))


def away_kernel(blocks, orders, feat_ref, act_ref, grad_ref, *refs):
    out_ref, q_ref = refs[blocks:]
    gather_factors(refs[:blocks], q_ref)
    for j in range(8):
        p_in, p_out = project(act_ref, grad_ref, q_ref, block_of(feat_ref[0], orders, j, 1))
        put(out_ref, j, jnp.concatenate([p_in, p_out], axis=0))


def home_kernel(blocks, orders, feat_ref, act_ref, grad_ref, *refs):
    got_ref, send_ref, keep_ref, q_ref = refs[blocks:]
    gather_factors(refs[:blocks], q_ref)
    for j in (4, 5, 6, 7, 0, 1, 2, 3):
        p_in, p_out = project(act_ref, grad_ref, q_ref, block_of(feat_ref[0], orders, j, 0))
        total = jnp.concatenate([p_in, p_out], axis=0) + get(got_ref, j)
        if j >= 4:
            put(send_ref, j - 4, total)
        else:
            keep_ref[j] = total


def step_kernel(keep_ref, got_ref, send_ref, left_ref):
    half = left_ref.shape[0]
    for pos in range(half):
        put(send_ref, pos, keep_ref[half + pos] + get(got_ref, half + pos))
    for pos in range(half):
        left_ref[pos] = keep_ref[pos] + get(got_ref, pos)


def last_kernel(tok_ref, *refs):
    out_ref = refs[-1]
    tok = tok_ref[0]
    for c, names in enumerate(CHUNKS):
        keep_ref, got_ref = refs[2 * c : 2 * c + 2]
        total = keep_ref[0] + get(got_ref, 0)
        half = total.shape[0] // 2
        product = (total[:half] * total[half:]).reshape(half // RANK, RANK, BLOCK)
        score = jnp.sum(product, axis=1)
        per = score.shape[0] // len(names)
        for i, name in enumerate(names):
            flip, turn = OWNERS[name]
            owner = ((tok & 4) ^ flip) | ((tok + turn) & 3)
            for k in range(per):
                out_ref[pl.ds(owner * per + k, 1), :] = score[i * per + k : i * per + k + 1, :]


def call(kernel, shapes, operands, flops=0, transcendentals=0, scalars=1, scratch=(), after=None, name=None):
    moved = sum(o.size * o.dtype.itemsize for o in operands)
    specs = [IN_SMEM] * scalars + [IN_VMEM] * (len(operands) - scalars)
    if after is not None:
        inner, place = kernel, len(operands)
        kernel = lambda *refs: inner(*refs[:place], *refs[place + 1 :])
        operands, specs = (*operands, after), [*specs, pl.BlockSpec(memory_space=pl.ANY)]
    return pl.pallas_call(
        kernel,
        in_specs=specs,
        out_specs=jax.tree.map(lambda _: IN_VMEM, shapes),
        out_shape=shapes,
        scratch_shapes=scratch,
        name=name,
        compiler_params=pltpu.CompilerParams(vmem_limit_bytes=VMEM),
        cost_estimate=pl.CostEstimate(flops=flops, transcendentals=0, bytes_accessed=1024),
    )(*operands)


def sends(count, rows):
    return [jax.ShapeDtypeStruct((count, rows + 16, BLOCK), jnp.bfloat16),
            jax.ShapeDtypeStruct((count, rows, BLOCK), jnp.float32)]


def local(activations, out_grads, query_in, query_out):
    per, rank, k_in = query_in.shape
    feat = jnp.reshape(lax.axis_index("feat"), (1,)).astype(jnp.int32)
    tok = jnp.reshape(lax.axis_index("tok"), (1,)).astype(jnp.int32)
    pairs = {
        "up": [(s, (s & 4) | ((s + 1) & 3)) for s in range(8)],
        "down": [(s, (s & 4) | ((s + 3) & 3)) for s in range(8)],
        "across": [(s, s ^ 4) for s in range(8)],
    }
    move = lambda value, way: lax.ppermute(value, "tok", pairs[way])

    own = pack(query_in.reshape(per * rank, -1), query_out.reshape(per * rank, -1))
    factor = {"own": own, "own_up": move(own, "up"), "own_down": move(own, "down"), "far": move(own, "across")}
    acts, grads = load((activations, out_grads))
    turn = {"after": None}
    got, keep = {}, {}

    def away(c):
        blocks = [factor[name] for name in CHUNKS[c]]
        side, width = sum(b.shape[0] for b in blocks), own.shape[1]
        scratch = [pltpu.VMEM((side, width), jnp.bfloat16)]
        send = call(functools.partial(away_kernel, len(blocks), ORDERS[c]), sends(8, 2 * side)[0],
                    (feat, acts, grads, *blocks), COST_OF.get(f"away_{c}", 1024), 0, 1, scratch, name=f"away_{c}", **turn)
        turn["after"] = send
        got[c] = lax.ppermute(send, "feat", [(s, s ^ 1) for s in range(16)])

    def home(c):
        blocks = [factor[name] for name in CHUNKS[c]]
        side, width = sum(b.shape[0] for b in blocks), own.shape[1]
        scratch = [pltpu.VMEM((side, width), jnp.bfloat16)]
        send, keep[c] = call(functools.partial(home_kernel, len(blocks), ORDERS[c]), sends(4, 2 * side),
                             (feat, acts, grads, *blocks, got[c]), COST_OF.get(f"home_{c}", 1024), 0, 1, scratch, name=f"home_{c}", **turn)
        turn["after"] = send
        got[c] = halve(send, ORDERS[c], 0)

    def step(c, stage):
        count, rows = keep[c].shape[:2]
        send, keep[c] = call(step_kernel, sends(count // 2, rows), (keep[c], got[c]),
                             COST_OF.get(f"step_{c}_{stage}", 1024), 0, 0, name=f"step_{c}_{stage}", **turn)
        turn["after"] = send
        got[c] = halve(send, ORDERS[c], stage)

    factor["own_two"] = move(factor["own_up"], "up")
    factor["far_down"] = move(factor["far"], "down")
    factor["far_up"] = move(factor["own_up"], "across")
    for item in PLAN:
        kind, c = item[0], item[1]
        if kind == "away":
            away(c)
        elif kind == "home":
            home(c)
        elif kind == "pass":
            ahead, _ = lax.optimization_barrier((factor["own_two"], turn["after"]))
            factor["far_two"] = move(ahead, "across")
        else:
            step(c, item[2])
    ends = [x for c in range(len(CHUNKS)) for x in (keep[c], got[c])]
    return call(last_kernel, jax.ShapeDtypeStruct((per * lax.axis_size("tok"), BLOCK), jnp.float32), (tok, *ends))


def solution(mesh):
    in_specs = (P("tok", "feat"), P("tok", "feat"), P("tok", None, "feat"), P("tok", None, "feat"))
    out_specs = P(None, ("tok", "feat"))
    return jax.shard_map(local, mesh=mesh, in_specs=in_specs, out_specs=out_specs, check_vma=False)
```
